512 devices in a mesh: leaf: 128 (over x, y_hi, z, core), col: 4 (over y_lo).
Axes of the slice: x: 4, y: 8 (y_hi: 2, y_lo: 4; y = y_hi * 4 + y_lo), z: 8, core: 2. Of those that a mesh axis runs over, the one named last changes fastest.
Arguments:
- leaf_inverse: float32 [256, 1024, 1024], P('leaf', 'col'), may hold values from -1 to 3, as said below
- left_gen: float32 [256, 1024, 256], P('leaf', 'col'), may hold values from -0.125 to 0.125
- right_gen: float32 [256, 1024, 256], P('leaf', 'col'), may hold values from -0.125 to 0.125
- parent_gen: float32 [256, 1024, 256], P('leaf', 'col'), may hold values from -6 to 6
Outputs:
- updated_gen: float32 [256, 1024, 256], P('leaf', 'col')
The draws below stay inside these ranges and needn't reach their ends.
Inputs may be any that keep to these rules, and one draw needn't show every extreme that they name: `leaf_inverse`: the inverse of a leaf block of the kernel matrix, of full rank.
All inputs are finite; a program needn't handle non-finite values.
Results may differ from the reference program's by a relative error of at most 0.000076.
Values sent between devices are 32-bit elements; how exact they have to be, the bound alone decides.
No kernel may reach another device: no remote copies, remote signals or barrier semaphores. Data moves between devices by JAX's collectives and lax.ppermute only.
A program may use at most 64 MiB of HBM per device.

```python
import jax
import jax.numpy as jnp
from jax import lax

M = 1024
K = 256
LEVEL = 2
LEAF_DEV = 2
LEAVES = 256


def draw_leaf_inverse(key, part):
    key = jax.random.fold_in(key, 11)
    first, second = jax.random.split(key)
    indices = jnp.arange(M, dtype=jnp.int32)
    diagonal_mask = (indices[:, None] == indices[None, :]).astype(jnp.float32)
    spread = 0.5 * jax.random.normal(first, (LEAVES, M, M), jnp.float32)
    height = jax.random.uniform(second, (LEAVES, M, 1), jnp.float32, 0.6, 1.6)
    return spread / jnp.sqrt(jnp.float32(M)) + diagonal_mask * height


def block_levels(key, extent, pieces, smallest, high):
    def one(position, shards_of):
        heights = jax.random.uniform(jax.random.fold_in(jax.random.fold_in(key, 6), position), (shards_of,), jnp.float32, smallest / len(pieces), high / len(pieces))
        return jnp.repeat(jnp.exp(heights), extent[position] // shards_of).reshape((-1,) + (1,) * (len(extent) - position - 1))

    level = one(*pieces[0])
    for cut in pieces[1:]:
        level = level * one(*cut)
    return level


def bell_draw(own_key, dims, width, bound, cuts=(), kind=jnp.bfloat16):
    loudness = block_levels(own_key, dims, cuts, -0.22, 0.18) if cuts else 1.0
    values = jax.random.normal(own_key, dims, jnp.float32) * width * loudness
    return jnp.minimum(jnp.maximum(values, -bound), bound).astype(kind)


def setup_inputs(seed: int = 0) -> dict:
    streams_of = jax.random.split(jax.random.key(seed), 5)
    return {
        "leaf_inverse": draw_leaf_inverse(jax.random.fold_in(streams_of[4], 71), 0),
        "left_gen": bell_draw(streams_of[1], (LEAVES, M, K), (2 * M) ** -0.5, 0.125, ((0, 128), (1, 4)), jnp.float32),
        "right_gen": bell_draw(streams_of[2], (LEAVES, M, K), (2 * M) ** -0.5, 0.125, ((0, 128), (1, 4)), jnp.float32),
        "parent_gen": bell_draw(streams_of[3], (LEAVES, M, K), 1.0, 6.0, ((0, 128), (1, 4)), jnp.float32),
    }


def reference(leaf_inverse, left_gen, right_gen, parent_gen):
    precise = lax.Precision.HIGHEST
    solved_left = jnp.einsum('lrm,lmk->lrk', leaf_inverse, left_gen, precision=precise)
    solved_parent = jnp.einsum('lrm,lmk->lrk', leaf_inverse, parent_gen, precision=precise)
    coupling = jnp.einsum('lrk,lrj->lkj', right_gen, solved_left, precision=precise)
    projected = jnp.einsum('lrk,lrj->lkj', right_gen, solved_parent, precision=precise)
    stride = LEAF_DEV * 2 ** LEVEL
    partner = jnp.bitwise_xor(jnp.arange(LEAVES, dtype=jnp.int32), jnp.int32(stride)).astype(jnp.int32)
    sibling_g = jnp.take(coupling, partner, axis=0)
    sibling_h = jnp.take(projected, partner, axis=0)
    reduced = jnp.eye(K, dtype=jnp.float32) - jnp.einsum('lab,lbc->lac', sibling_g, coupling, precision=precise)
    target = sibling_h - jnp.einsum('lab,lbc->lac', sibling_g, projected, precision=precise)
    coeffs = jnp.linalg.solve(reduced, target)
    return solved_parent - jnp.einsum('lrk,lkj->lrj', solved_left, coeffs, precision=precise)
```

```python
import functools

import jax
import jax.numpy as jnp
from jax import lax
from jax.experimental import pallas as pl
from jax.experimental.pallas import tpu as pltpu
from jax.sharding import PartitionSpec as P

LEVEL = 2
RUN = 4
NN = (((1,), (0,)), ((), ()))
NT = (((1,), (1,)), ((), ()))
TN = (((0,), (0,)), ((), ()))
PARAMS = pltpu.CompilerParams(vmem_limit_bytes=40 * 1024 * 1024)
SETTLED = 2.4e-4
DOUBLINGS = 9


def split(value):
    high = value.astype(jnp.bfloat16)
    low = (value - high.astype(jnp.float32)).astype(jnp.bfloat16)
    return high, low


def dot3(left, right, dims=NN):
    product = functools.partial(
        lax.dot_general, dimension_numbers=dims, preferred_element_type=jnp.float32
    )
    (lh, ll), (rh, rl) = left, right
    return product(lh, rh) + (product(lh, rl) + product(ll, rh))


def mul(left, right, dims=NN):
    return dot3(split(left), split(right), dims)


def exact(left, right, dims=NN):
    return lax.dot_general(
        left, right, dims, precision=lax.Precision.HIGHEST, preferred_element_type=jnp.float32
    )


def apply_kernel(place, inverse, right, own, left0, right0, left1, right1, left2, right2, solved, small):
    c = place[0]
    rows = own.shape[1]
    inner = jnp.logical_and(c >= 1, c <= RUN - 2)
    for leaf in range(own.shape[0]):
        blocks = (
            (c, own[leaf]),
            (jnp.where(c >= 2, c - 2, c + 2), left1[leaf] + right1[leaf]),
            (jnp.where(c >= 1, c - 1, c + 1), jnp.where(c >= 1, left0[leaf], right0[leaf])),
            (
                jnp.where(inner, c + 1, RUN - 1 - c),
                jnp.where(inner, right0[leaf], left2[leaf] + right2[leaf]),
            ),
        )
        total = None
        for index, block in blocks:
            columns = pl.ds(pl.multiple_of(index * rows, rows), rows)
            term = mul(inverse[leaf, :, columns], block)
            total = term if total is None else total + term
        solved[leaf] = total
        small[leaf] = mul(total, right[leaf], TN)


def apply_gathered(place, inverse, right, blocks):
    own = blocks[0]
    leaves, rows, order_k = own.shape
    vmem = pl.BlockSpec(memory_space=pltpu.VMEM)
    return pl.pallas_call(
        apply_kernel,
        out_shape=(
            jax.ShapeDtypeStruct((leaves, inverse.shape[1], order_k), jnp.float32),
            jax.ShapeDtypeStruct((leaves, order_k, order_k), jnp.float32),
        ),
        in_specs=[pl.BlockSpec(memory_space=pltpu.SMEM)] + [vmem] * 9,
        out_specs=(vmem, vmem),
        compiler_params=PARAMS,
        cost_estimate=pl.CostEstimate(
            flops=10 * leaves * rows * order_k * rows * 3, bytes_accessed=6 << 20, transcendentals=0
        ),
        name="apply",
    )(place, inverse, right, *blocks)


def eliminate(matrix, joined):
    size = matrix.shape[0]
    row = lax.broadcasted_iota(jnp.int32, (size, size), 0)
    lane = lax.broadcasted_iota(jnp.int32, (size, size), 1)
    identity = (row == lane).astype(jnp.float32)
    joined[0] = matrix
    joined[1] = identity
    tall = lax.broadcasted_iota(jnp.int32, (size, 1), 0)

    def step(k, carry):
        used, picks = carry
        left = joined[0]
        column = jnp.sum(jnp.where(lane == k, left, 0.0), axis=1, keepdims=True)
        height = jnp.where(used > 0.0, -1.0, jnp.abs(column))
        best = jnp.max(height, axis=0, keepdims=True)
        pick = jnp.min(jnp.where(height == best, tall, size), axis=0, keepdims=True)
        chosen = tall == pick
        pivot = jnp.sum(jnp.where(chosen, column, 0.0), axis=0, keepdims=True)
        others = jnp.where(chosen, 0.0, column)
        for side in range(2):
            part = joined[side]
            pivot_row = jnp.sum(jnp.where(chosen, part, 0.0), axis=0, keepdims=True) / pivot
            joined[side] = jnp.where(chosen, pivot_row, part - others * pivot_row)
        picks = jnp.where(jnp.logical_and(chosen, lane == k), 1.0, picks)
        return jnp.where(chosen, 1.0, used), picks

    _, picks = lax.fori_loop(
        0, size, step, (jnp.zeros((size, 1), jnp.float32), jnp.zeros((size, size), jnp.float32))
    )
    return exact(picks, joined[1], TN)


def invert_kernel(gathered, inverse, power, joined):
    size = inverse.shape[0]
    first = gathered[:, 0].reshape(size, size)
    second = gathered[:, 1].reshape(size, size)
    row = lax.broadcasted_iota(jnp.int32, (size, size), 0)
    lane = lax.broadcasted_iota(jnp.int32, (size, size), 1)
    identity = (row == lane).astype(jnp.float32)
    start = exact(first, second)
    power[...] = start
    inverse[...] = identity + start

    def unsettled(state):
        count, norm = state
        going = jnp.logical_and(norm > SETTLED * SETTLED, norm < 1e12)
        return jnp.logical_and(count < DOUBLINGS, going)

    def double(state):
        count, _ = state
        current = split(power[...])
        square = dot3(current, current)
        power[...] = square
        held = inverse[...]
        inverse[...] = held + mul(held, square)
        return count + 1, jnp.sum(square * square)

    _, norm = lax.while_loop(unsettled, double, (jnp.int32(0), jnp.sum(start * start)))

    @pl.when(jnp.logical_not(norm <= SETTLED * SETTLED))
    def _():
        inverse[...] = eliminate(identity - exact(first, second), joined)


def invert(gathered):
    size = gathered.shape[-1]
    vmem = pl.BlockSpec(memory_space=pltpu.VMEM)
    return pl.pallas_call(
        invert_kernel,
        out_shape=jax.ShapeDtypeStruct((size, size), jnp.float32),
        in_specs=[vmem],
        out_specs=vmem,
        scratch_shapes=[
            pltpu.VMEM((size, size), jnp.float32),
            pltpu.VMEM((2, size, size), jnp.float32),
        ],
        compiler_params=PARAMS,
        cost_estimate=pl.CostEstimate(
            flops=10 * 6 * size**3, bytes_accessed=1 << 20, transcendentals=0
        ),
        name="invert",
    )(gathered)


def coeffs_kernel(pieces, gathered, inverse, sent):
    size = inverse.shape[0]
    first = gathered[:, 0].reshape(size, size)
    second = gathered[:, 1].reshape(size, size)
    first_h = pieces[0] + pieces[1] + (pieces[2] + pieces[3])
    second_h = pieces[4] + pieces[5] + (pieces[6] + pieces[7])
    target = second_h - mul(first_h, second)
    first_c = mul(target, inverse[...])
    second_c = first_h - mul(first_c, first)
    for q in range(RUN):
        sent[q] = first_c
        sent[RUN + q] = second_c


def coeffs(pieces, gathered, inverse):
    vmem = pl.BlockSpec(memory_space=pltpu.VMEM)
    return pl.pallas_call(
        coeffs_kernel,
        out_shape=jax.ShapeDtypeStruct(pieces.shape, jnp.float32),
        in_specs=[vmem] * 3,
        out_specs=vmem,
        compiler_params=PARAMS,
        name="coeffs",
    )(pieces, gathered, inverse)


def final_kernel(second, first, coeffs_t, out):
    for leaf in range(out.shape[0]):
        out[leaf] = second[leaf] - mul(first[leaf], coeffs_t[leaf], NT)


def final(second, first, coeffs_t):
    vmem = pl.BlockSpec(memory_space=pltpu.VMEM)
    return pl.pallas_call(
        final_kernel,
        out_shape=jax.ShapeDtypeStruct(second.shape, jnp.float32),
        in_specs=[vmem] * 3,
        out_specs=vmem,
        compiler_params=PARAMS,
        name="final",
    )(second, first, coeffs_t)


def hop(shard, direction, step):
    if direction > 0:
        pairs = [(i, i + 1) for i in range(step, RUN - 1)]
    else:
        pairs = [(i + 1, i) for i in range(0, RUN - 1 - step)]
    return lax.ppermute(shard, "col", pairs)


def body(leaf_inverse, left_gen, right_gen, parent_gen):
    leaves, rows, order_k = left_gen.shape
    quarter = order_k // RUN
    place = lax.axis_index("col").reshape(1).astype(jnp.int32)
    stride = 1 << LEVEL
    groups = [
        [side * RUN + q for side in (leaf, leaf ^ stride) for q in range(RUN)]
        for leaf in range(lax.axis_size("leaf"))
        if not leaf & stride
    ]

    def exchange(value):
        return lax.all_to_all(value, ("leaf", "col"), 0, 0, axis_index_groups=groups, tiled=True)

    def gather(own, after=None):
        blocks = [own]
        onward = back = own
        for step in range(RUN - 1):
            onward, back = hop(onward, 1, step), hop(back, -1, step)
            blocks += [onward, back]
        return blocks

    left_blocks = gather(left_gen)
    parent_start, _ = lax.optimization_barrier((parent_gen, left_blocks[3]))
    parent_blocks = gather(parent_start)

    first, small_g = apply_gathered(place, leaf_inverse, right_gen, left_blocks)
    pieces = exchange(small_g.reshape(2 * RUN, quarter, order_k))
    summed = jnp.sum(pieces.reshape(2, RUN, quarter, order_k), axis=1)
    gathered = lax.all_to_all(
        jnp.broadcast_to(summed, (RUN,) + summed.shape), "col", 0, 0, tiled=True
    )
    inverse = invert(gathered)

    second, small_h = apply_gathered(place, leaf_inverse, right_gen, parent_blocks)
    pieces_h = exchange(small_h.reshape(2 * RUN, quarter, order_k))
    sent = coeffs(pieces_h, gathered, inverse)
    coeffs_t = exchange(sent).reshape(leaves, order_k, order_k)
    return final(second, first, coeffs_t)


def solution(mesh):
    return jax.shard_map(
        body,
        mesh=mesh,
        in_specs=(
            P("leaf", "col", None),
            P("leaf", "col", None),
            P("leaf", "col", None),
            P("leaf", "col", None),
        ),
        out_specs=P("leaf", "col", None),
        check_vma=False,
    )
```

```python
import functools

import jax
import jax.numpy as jnp
from jax import lax
from jax.experimental import pallas as pl
from jax.experimental.pallas import tpu as pltpu
from jax.sharding import PartitionSpec as P

LEVEL = 2
RUN = 4
NN = (((1,), (0,)), ((), ()))
NT = (((1,), (1,)), ((), ()))
TN = (((0,), (0,)), ((), ()))
PARAMS = pltpu.CompilerParams(vmem_limit_bytes=40 * 1024 * 1024)
SETTLED = 2.4e-4
DOUBLINGS = 9
WEIGHT = 40


def split(value):
    high = value.astype(jnp.bfloat16)
    low = (value - high.astype(jnp.float32)).astype(jnp.bfloat16)
    return high, low


def dot3(left, right, dims=NN):
    product = functools.partial(
        lax.dot_general, dimension_numbers=dims, preferred_element_type=jnp.float32
    )
    (lh, ll), (rh, rl) = left, right
    return product(lh, rh) + (product(lh, rl) + product(ll, rh))


def mul(left, right, dims=NN):
    return dot3(split(left), split(right), dims)


def exact(left, right, dims=NN):
    return lax.dot_general(
        left, right, dims, precision=lax.Precision.HIGHEST, preferred_element_type=jnp.float32
    )


def near_kernel(place, inverse, own, left0, right0, left1, right1, partial, far_high, far_low):
    c = place[0]
    rows = own.shape[1]
    inner = jnp.logical_and(c >= 1, c <= RUN - 2)

    def columns(index):
        return pl.ds(pl.multiple_of(index * rows, rows), rows)

    for leaf in range(own.shape[0]):
        total = mul(inverse[leaf, :, columns(c)], own[leaf])
        second = jnp.where(c >= 2, c - 2, c + 2)
        total += mul(inverse[leaf, :, columns(second)], left1[leaf] + right1[leaf])
        third = jnp.where(c >= 1, c - 1, c + 1)
        block = jnp.where(c >= 1, left0[leaf], right0[leaf])
        total += mul(inverse[leaf, :, columns(third)], block)
        partial[leaf] = total
        far = inverse[leaf, :, columns(jnp.where(inner, c + 1, RUN - 1 - c))]
        far_high[leaf], far_low[leaf] = split(far)

    @pl.when(inner)
    def _():
        for leaf in range(own.shape[0]):
            far = (far_high[leaf], far_low[leaf])
            partial[leaf] += dot3(far, split(right0[leaf]))
            far_high[leaf] = jnp.zeros_like(far_high[leaf])
            far_low[leaf] = jnp.zeros_like(far_low[leaf])


def near(place, inverse, blocks, weight=1):
    leaves, rows, order_k = blocks[0].shape
    vmem = pl.BlockSpec(memory_space=pltpu.VMEM)
    return pl.pallas_call(
        near_kernel,
        out_shape=(
            jax.ShapeDtypeStruct((leaves, rows, order_k), jnp.float32),
            jax.ShapeDtypeStruct((leaves, rows, rows), jnp.bfloat16),
            jax.ShapeDtypeStruct((leaves, rows, rows), jnp.bfloat16),
        ),
        in_specs=[pl.BlockSpec(memory_space=pltpu.SMEM)] + [vmem] * 6,
        out_specs=(vmem,) * 3,
        compiler_params=PARAMS,
        cost_estimate=pl.CostEstimate(
            flops=weight * 8 * leaves * rows * order_k * rows * 3,
            bytes_accessed=6 << 20,
            transcendentals=0,
        ),
        name="near",
    )(place, inverse, *blocks)


def far_kernel(partial, far_high, far_low, left2, right2, right, solved, small):
    for leaf in range(partial.shape[0]):
        block = left2[leaf] + right2[leaf]
        total = partial[leaf] + dot3((far_high[leaf], far_low[leaf]), split(block))
        solved[leaf] = total
        small[leaf] = mul(total, right[leaf], TN)


def far(partial, far_high, far_low, left2, right2, right, weight=1):
    leaves, rows, order_k = partial.shape
    vmem = pl.BlockSpec(memory_space=pltpu.VMEM)
    return pl.pallas_call(
        far_kernel,
        out_shape=(
            jax.ShapeDtypeStruct(partial.shape, jnp.float32),
            jax.ShapeDtypeStruct((leaves, order_k, order_k), jnp.float32),
        ),
        in_specs=[vmem] * 6,
        out_specs=(vmem,) * 2,
        compiler_params=PARAMS,
        cost_estimate=pl.CostEstimate(
            flops=weight * 4 * leaves * rows * order_k * rows * 3,
            bytes_accessed=3 << 20,
            transcendentals=0,
        ),
        name="far",
    )(partial, far_high, far_low, left2, right2, right)


def spread_kernel(pieces, sent):
    for side in range(2):
        p = RUN * side
        total = pieces[p] + pieces[p + 1] + (pieces[p + 2] + pieces[p + 3])
        for q in range(RUN):
            sent[q, side] = total


def spread(pieces):
    vmem = pl.BlockSpec(memory_space=pltpu.VMEM)
    return pl.pallas_call(
        spread_kernel,
        out_shape=jax.ShapeDtypeStruct((RUN, 2) + pieces.shape[1:], jnp.float32),
        in_specs=[vmem],
        out_specs=vmem,
        compiler_params=PARAMS,
        name="spread",
    )(pieces)


def eliminate(matrix, joined):
    size = matrix.shape[0]
    row = lax.broadcasted_iota(jnp.int32, (size, size), 0)
    lane = lax.broadcasted_iota(jnp.int32, (size, size), 1)
    identity = (row == lane).astype(jnp.float32)
    joined[0] = matrix
    joined[1] = identity
    tall = lax.broadcasted_iota(jnp.int32, (size, 1), 0)

    def step(k, carry):
        used, picks = carry
        left = joined[0]
        column = jnp.sum(jnp.where(lane == k, left, 0.0), axis=1, keepdims=True)
        height = jnp.where(used > 0.0, -1.0, jnp.abs(column))
        best = jnp.max(height, axis=0, keepdims=True)
        pick = jnp.min(jnp.where(height == best, tall, size), axis=0, keepdims=True)
        chosen = tall == pick
        pivot = jnp.sum(jnp.where(chosen, column, 0.0), axis=0, keepdims=True)
        others = jnp.where(chosen, 0.0, column)
        for side in range(2):
            part = joined[side]
            pivot_row = jnp.sum(jnp.where(chosen, part, 0.0), axis=0, keepdims=True) / pivot
            joined[side] = jnp.where(chosen, pivot_row, part - others * pivot_row)
        picks = jnp.where(jnp.logical_and(chosen, lane == k), 1.0, picks)
        return jnp.where(chosen, 1.0, used), picks

    _, picks = lax.fori_loop(
        0, size, step, (jnp.zeros((size, 1), jnp.float32), jnp.zeros((size, size), jnp.float32))
    )
    return exact(picks, joined[1], TN)


def invert_kernel(gathered, inverse, power, joined):
    size = inverse.shape[0]
    first = gathered[:, 0].reshape(size, size)
    second = gathered[:, 1].reshape(size, size)
    row = lax.broadcasted_iota(jnp.int32, (size, size), 0)
    lane = lax.broadcasted_iota(jnp.int32, (size, size), 1)
    identity = (row == lane).astype(jnp.float32)
    start = exact(first, second)
    power[...] = start
    inverse[...] = identity + start

    def unsettled(state):
        count, norm = state
        going = jnp.logical_and(norm > SETTLED * SETTLED, norm < 1e12)
        return jnp.logical_and(count < DOUBLINGS, going)

    def double(state):
        count, _ = state
        current = split(power[...])
        square = dot3(current, current)
        power[...] = square
        held = inverse[...]
        inverse[...] = held + mul(held, square)
        return count + 1, jnp.sum(square * square)

    _, norm = lax.while_loop(unsettled, double, (jnp.int32(0), jnp.sum(start * start)))

    @pl.when(jnp.logical_not(norm <= SETTLED * SETTLED))
    def _():
        inverse[...] = eliminate(identity - exact(first, second), joined)


def invert(gathered):
    size = gathered.shape[-1]
    vmem = pl.BlockSpec(memory_space=pltpu.VMEM)
    return pl.pallas_call(
        invert_kernel,
        out_shape=jax.ShapeDtypeStruct((size, size), jnp.float32),
        in_specs=[vmem],
        out_specs=vmem,
        scratch_shapes=[
            pltpu.VMEM((size, size), jnp.float32),
            pltpu.VMEM((2, size, size), jnp.float32),
        ],
        compiler_params=PARAMS,
        cost_estimate=pl.CostEstimate(
            flops=10 * 6 * size**3, bytes_accessed=1 << 20, transcendentals=0
        ),
        name="invert",
    )(gathered)


def coeffs_kernel(pieces, gathered, inverse, sent):
    size = inverse.shape[0]
    first = gathered[:, 0].reshape(size, size)
    second = gathered[:, 1].reshape(size, size)
    first_h = pieces[0] + pieces[1] + (pieces[2] + pieces[3])
    second_h = pieces[4] + pieces[5] + (pieces[6] + pieces[7])
    target = second_h - mul(first_h, second)
    first_c = mul(target, inverse[...])
    second_c = first_h - mul(first_c, first)
    for q in range(RUN):
        sent[q] = first_c
        sent[RUN + q] = second_c


def coeffs(pieces, gathered, inverse):
    vmem = pl.BlockSpec(memory_space=pltpu.VMEM)
    return pl.pallas_call(
        coeffs_kernel,
        out_shape=jax.ShapeDtypeStruct(pieces.shape, jnp.float32),
        in_specs=[vmem] * 3,
        out_specs=vmem,
        compiler_params=PARAMS,
        name="coeffs",
    )(pieces, gathered, inverse)


def final_kernel(second, first, coeffs_t, out):
    for leaf in range(out.shape[0]):
        out[leaf] = second[leaf] - mul(first[leaf], coeffs_t[leaf], NT)


def final(second, first, coeffs_t):
    vmem = pl.BlockSpec(memory_space=pltpu.VMEM)
    return pl.pallas_call(
        final_kernel,
        out_shape=jax.ShapeDtypeStruct(second.shape, jnp.float32),
        in_specs=[vmem] * 3,
        out_specs=vmem,
        compiler_params=PARAMS,
        name="final",
    )(second, first, coeffs_t)


def hop(shard, direction, step):
    if direction > 0:
        pairs = [(i, i + 1) for i in range(step, RUN - 1)]
    else:
        pairs = [(i + 1, i) for i in range(0, RUN - 1 - step)]
    return lax.ppermute(shard, "col", pairs)


def body(leaf_inverse, left_gen, right_gen, parent_gen):
    leaves, rows, order_k = left_gen.shape
    quarter = order_k // RUN
    place = lax.axis_index("col").reshape(1).astype(jnp.int32)
    stride = 1 << LEVEL
    groups = [
        [side * RUN + q for side in (leaf, leaf ^ stride) for q in range(RUN)]
        for leaf in range(lax.axis_size("leaf"))
        if not leaf & stride
    ]

    def exchange(value):
        return lax.all_to_all(value, ("leaf", "col"), 0, 0, axis_index_groups=groups, tiled=True)

    def hops(onward, back, step):
        return hop(onward, 1, step), hop(back, -1, step)

    left0 = hops(left_gen, left_gen, 0)
    parent0 = hops(parent_gen, parent_gen, 0)
    left1 = hops(*left0, 1)
    left1, parent0 = lax.optimization_barrier((left1, parent0))
    left2 = hops(*left1, 2)
    parent1 = hops(*parent0, 1)
    partial, *far_columns = near(place, leaf_inverse, (left_gen, *left0, *left1))
    first, small_g = far(partial, *far_columns, *left2, right_gen)
    parent2 = hops(*parent1, 2)

    pieces = exchange(small_g.reshape(2 * RUN, quarter, order_k))
    gathered = lax.all_to_all(spread(pieces), "col", 0, 0, tiled=True)
    inverse = invert(gathered)

    partial_h, *far_columns = near(place, leaf_inverse, (parent_gen, *parent0, *parent1), WEIGHT)
    second, small_h = far(partial_h, *far_columns, *parent2, right_gen, WEIGHT)
    pieces_h = exchange(small_h.reshape(2 * RUN, quarter, order_k))
    sent = coeffs(pieces_h, gathered, inverse)
    coeffs_t = exchange(sent).reshape(leaves, order_k, order_k)
    return final(second, first, coeffs_t)


def solution(mesh):
    return jax.shard_map(
        body,
        mesh=mesh,
        in_specs=(
            P("leaf", "col", None),
            P("leaf", "col", None),
            P("leaf", "col", None),
            P("leaf", "col", None),
        ),
        out_specs=P("leaf", "col", None),
        check_vma=False,
    )
```

```python
import functools

import jax
import jax.numpy as jnp
from jax import lax
from jax.experimental import pallas as pl
from jax.experimental.pallas import tpu as pltpu
from jax.sharding import PartitionSpec as P

LEVEL = 2
RUN = 4
NN = (((1,), (0,)), ((), ()))
NT = (((1,), (1,)), ((), ()))
TN = (((0,), (0,)), ((), ()))
PARAMS = pltpu.CompilerParams(vmem_limit_bytes=16 * 1024 * 1024)
SETTLED = 2.4e-4
DOUBLINGS = 9
WEIGHT = 40


def split(value):
    high = value.astype(jnp.bfloat16)
    low = (value - high.astype(jnp.float32)).astype(jnp.bfloat16)
    return high, low


def dot3(left, right, dims=NN):
    product = functools.partial(
        lax.dot_general, dimension_numbers=dims, preferred_element_type=jnp.float32
    )
    (lh, ll), (rh, rl) = left, right
    return product(lh, rh) + (product(lh, rl) + product(ll, rh))


def mul(left, right, dims=NN):
    return dot3(split(left), split(right), dims)


def exact(left, right, dims=NN):
    return lax.dot_general(
        left, right, dims, precision=lax.Precision.HIGHEST, preferred_element_type=jnp.float32
    )


def call(kernel, name, shapes, operands, flops, scalars=0, scratch=()):
    vmem = pl.BlockSpec(memory_space=pltpu.VMEM)
    smem = pl.BlockSpec(memory_space=pltpu.SMEM)
    return pl.pallas_call(
        kernel,
        out_shape=tuple(jax.ShapeDtypeStruct(shape, dtype) for shape, dtype in shapes),
        in_specs=[smem] * scalars + [vmem] * (len(operands) - scalars),
        out_specs=(vmem,) * len(shapes),
        scratch_shapes=list(scratch),
        compiler_params=PARAMS,
        cost_estimate=pl.CostEstimate(flops=flops, bytes_accessed=4 << 20, transcendentals=0),
        name=name,
    )(*operands)


def block_columns(c, rows):
    near_half = c < RUN // 2
    indices = (c, jnp.bitwise_xor(c, 1), jnp.where(near_half, 2, 1), jnp.where(near_half, 3, 0))
    return [pl.ds(pl.multiple_of(index * rows, rows), rows) for index in indices]


def near_kernel(place, inverse, own, inner0, end0, across0, end1, part, far_high, far_low):
    strips = block_columns(place[0], own.shape[1])
    for leaf in range(own.shape[0]):
        total = mul(inverse[leaf, :, strips[0]], own[leaf])
        total += mul(inverse[leaf, :, strips[1]], inner0[leaf] + end0[leaf])
        part[leaf] = total + mul(inverse[leaf, :, strips[2]], across0[leaf] + end1[leaf])
        far_high[leaf], far_low[leaf] = split(inverse[leaf, :, strips[3]])


def last_kernel(part, far_high, far_low, across1, end2, right, solved, small):
    for leaf in range(part.shape[0]):
        block = split(across1[leaf] + end2[leaf])
        total = part[leaf] + dot3((far_high[leaf], far_low[leaf]), block)
        solved[leaf] = total
        small[leaf] = mul(total, right[leaf], TN)


def spread_kernel(pieces, sent):
    for side in range(2):
        p = RUN * side
        total = pieces[p] + pieces[p + 1] + (pieces[p + 2] + pieces[p + 3])
        for q in range(RUN):
            sent[q, side] = total


def eliminate(matrix, joined):
    size = matrix.shape[0]
    row = lax.broadcasted_iota(jnp.int32, (size, size), 0)
    lane = lax.broadcasted_iota(jnp.int32, (size, size), 1)
    identity = (row == lane).astype(jnp.float32)
    joined[0] = matrix
    joined[1] = identity
    tall = lax.broadcasted_iota(jnp.int32, (size, 1), 0)

    def step(k, carry):
        used, picks = carry
        left = joined[0]
        column = jnp.sum(jnp.where(lane == k, left, 0.0), axis=1, keepdims=True)
        height = jnp.where(used > 0.0, -1.0, jnp.abs(column))
        best = jnp.max(height, axis=0, keepdims=True)
        pick = jnp.min(jnp.where(height == best, tall, size), axis=0, keepdims=True)
        chosen = tall == pick
        pivot = jnp.sum(jnp.where(chosen, column, 0.0), axis=0, keepdims=True)
        others = jnp.where(chosen, 0.0, column)
        for side in range(2):
            part = joined[side]
            pivot_row = jnp.sum(jnp.where(chosen, part, 0.0), axis=0, keepdims=True) / pivot
            joined[side] = jnp.where(chosen, pivot_row, part - others * pivot_row)
        picks = jnp.where(jnp.logical_and(chosen, lane == k), 1.0, picks)
        return jnp.where(chosen, 1.0, used), picks

    _, picks = lax.fori_loop(
        0, size, step, (jnp.zeros((size, 1), jnp.float32), jnp.zeros((size, size), jnp.float32))
    )
    return exact(picks, joined[1], TN)


def invert_kernel(gathered, inverse, power, joined):
    size = inverse.shape[0]
    first = gathered[:, 0].reshape(size, size)
    second = gathered[:, 1].reshape(size, size)
    row = lax.broadcasted_iota(jnp.int32, (size, size), 0)
    lane = lax.broadcasted_iota(jnp.int32, (size, size), 1)
    identity = (row == lane).astype(jnp.float32)
    start = exact(first, second)
    power[...] = start
    inverse[...] = identity + start

    def unsettled(state):
        count, norm = state
        going = jnp.logical_and(norm > SETTLED * SETTLED, norm < 1e12)
        return jnp.logical_and(count < DOUBLINGS, going)

    def double(state):
        count, _ = state
        current = split(power[...])
        square = dot3(current, current)
        power[...] = square
        held = inverse[...]
        inverse[...] = held + mul(held, square)
        return count + 1, jnp.sum(square * square)

    _, norm = lax.while_loop(unsettled, double, (jnp.int32(0), jnp.sum(start * start)))

    @pl.when(jnp.logical_not(norm <= SETTLED * SETTLED))
    def _():
        inverse[...] = eliminate(identity - exact(first, second), joined)


def coeffs_kernel(pieces, gathered, inverse, sent):
    size = inverse.shape[0]
    first = gathered[:, 0].reshape(size, size)
    second = gathered[:, 1].reshape(size, size)
    first_h = pieces[0] + pieces[1] + (pieces[2] + pieces[3])
    second_h = pieces[4] + pieces[5] + (pieces[6] + pieces[7])
    target = second_h - mul(first_h, second)
    first_c = mul(target, inverse[...])
    second_c = first_h - mul(first_c, first)
    for q in range(RUN):
        sent[q] = first_c
        sent[RUN + q] = second_c


def final_kernel(second, first, coeffs_t, out):
    for leaf in range(out.shape[0]):
        out[leaf] = second[leaf] - mul(first[leaf], coeffs_t[leaf], NT)


TO_INNER = [(0, 1), (RUN - 1, RUN - 2)]
TO_END = [(1, 0), (RUN - 2, RUN - 1)]
ACROSS = [(1, RUN - 2), (RUN - 2, 1)]


def move(shard, pairs):
    return lax.ppermute(shard, "col", pairs)


def body(leaf_inverse, left_gen, right_gen, parent_gen):
    leaves, rows, order_k = left_gen.shape
    quarter = order_k // RUN
    place = lax.axis_index("col").reshape(1).astype(jnp.int32)
    stride = 1 << LEVEL
    groups = [
        [side * RUN + q for side in (leaf, leaf ^ stride) for q in range(RUN)]
        for leaf in range(lax.axis_size("leaf"))
        if not leaf & stride
    ]
    f32, bf16 = jnp.float32, jnp.bfloat16
    both = ((leaves, rows, order_k), f32)
    small = ((leaves, order_k, order_k), f32)
    strips = ((leaves, rows, rows), bf16)
    square = ((order_k, order_k), f32)
    unit = 6 * rows * rows * order_k

    def exchange(value):
        return lax.all_to_all(value, ("leaf", "col"), 0, 0, axis_index_groups=groups, tiled=True)

    def near(weight, *gens):
        return call(
            near_kernel,
            "near",
            (both, strips, strips),
            (place, leaf_inverse) + gens,
            weight * 6 * unit,
            scalars=1,
        )

    def last(weight, parts, *gens):
        return call(
            last_kernel, "last", (both, small), (*parts, *gens, right_gen), weight * 4 * unit
        )

    inner0 = move(left_gen, TO_INNER)
    across0 = move(left_gen, ACROSS)
    end0 = move(left_gen, TO_END)
    inner0, across0, end0, parent = lax.optimization_barrier((inner0, across0, end0, parent_gen))
    across1 = move(inner0, ACROSS)
    end1 = move(across0, TO_END)
    inner0_p = move(parent, TO_INNER)
    across1, end1, parent = lax.optimization_barrier((across1, end1, parent))
    end2 = move(across1, TO_END)
    across0_p = move(parent, ACROSS)
    end0_p = move(parent, TO_END)
    near_g = near(1, left_gen, inner0, end0, across0, end1)
    first, small_g = last(1, near_g, across1, end2)

    across1_p = move(inner0_p, ACROSS)
    end1_p = move(across0_p, TO_END)
    end2_p = move(across1_p, TO_END)
    near_h = near(WEIGHT, parent_gen, inner0_p, end0_p, across0_p, end1_p)
    second, small_h = last(WEIGHT, near_h, across1_p, end2_p)

    pieces = exchange(small_g.reshape(2 * RUN, quarter, order_k))
    (spread,) = call(
        spread_kernel, "spread", (((RUN, 2, quarter, order_k), f32),), (pieces,), unit // 8
    )
    gathered = lax.all_to_all(spread, "col", 0, 0, tiled=True)
    (inverse,) = call(
        invert_kernel,
        "invert",
        (square,),
        (gathered,),
        10 * unit,
        scratch=(pltpu.VMEM(square[0], f32), pltpu.VMEM((2,) + square[0], f32)),
    )
    pieces_h = exchange(small_h.reshape(2 * RUN, quarter, order_k))
    (sent,) = call(
        coeffs_kernel, "coeffs", ((pieces_h.shape, f32),), (pieces_h, gathered, inverse), unit
    )
    coeffs_t = exchange(sent).reshape(leaves, order_k, order_k)
    (out,) = call(final_kernel, "final", (both,), (second, first, coeffs_t), 2 * unit)
    return out


def solution(mesh):
    return jax.shard_map(
        body,
        mesh=mesh,
        in_specs=(
            P("leaf", "col", None),
            P("leaf", "col", None),
            P("leaf", "col", None),
            P("leaf", "col", None),
        ),
        out_specs=P("leaf", "col", None),
        check_vma=False,
    )
```

```python
import functools

import jax
import jax.numpy as jnp
from jax import lax
from jax.experimental import pallas as pl
from jax.experimental.pallas import tpu as pltpu
from jax.sharding import PartitionSpec as P

LEVEL = 2
RUN = 4
NN = (((1,), (0,)), ((), ()))
NT = (((1,), (1,)), ((), ()))
TN = (((0,), (0,)), ((), ()))
PARAMS = pltpu.CompilerParams(vmem_limit_bytes=16 * 1024 * 1024)
SETTLED = 2.4e-4
DOUBLINGS = 9
WEIGHT = 40


def split(value):
    high = value.astype(jnp.bfloat16)
    low = (value - high.astype(jnp.float32)).astype(jnp.bfloat16)
    return high, low


def dot3(left, right, dims=NN):
    product = functools.partial(
        lax.dot_general, dimension_numbers=dims, preferred_element_type=jnp.float32
    )
    (lh, ll), (rh, rl) = left, right
    return product(lh, rh) + (product(lh, rl) + product(ll, rh))


def mul(left, right, dims=NN):
    return dot3(split(left), split(right), dims)


def exact(left, right, dims=NN):
    return lax.dot_general(
        left, right, dims, precision=lax.Precision.HIGHEST, preferred_element_type=jnp.float32
    )


def call(kernel, name, shapes, operands, flops, scalars=0, scratch=()):
    vmem = pl.BlockSpec(memory_space=pltpu.VMEM)
    smem = pl.BlockSpec(memory_space=pltpu.SMEM)
    return pl.pallas_call(
        kernel,
        out_shape=tuple(jax.ShapeDtypeStruct(shape, dtype) for shape, dtype in shapes),
        in_specs=[smem] * scalars + [vmem] * (len(operands) - scalars),
        out_specs=(vmem,) * len(shapes),
        scratch_shapes=list(scratch),
        compiler_params=PARAMS,
        cost_estimate=pl.CostEstimate(flops=flops, bytes_accessed=4 << 20, transcendentals=0),
        name=name,
    )(*operands)


def block_columns(c, rows):
    near_half = c < RUN // 2
    indices = (c, jnp.bitwise_xor(c, 1), jnp.where(near_half, 2, 1), jnp.where(near_half, 3, 0))
    return [pl.ds(pl.multiple_of(index * rows, rows), rows) for index in indices]


def fourth_kernel(place, inverse, far_high, far_low):
    strips = block_columns(place[0], inverse.shape[1])
    for leaf in range(inverse.shape[0]):
        far_high[leaf], far_low[leaf] = split(inverse[leaf, :, strips[3]])


def near_kernel(place, inverse, own, inner0, end0, across0, end1, part):
    strips = block_columns(place[0], own.shape[1])
    for leaf in range(own.shape[0]):
        total = mul(inverse[leaf, :, strips[0]], own[leaf])
        total += mul(inverse[leaf, :, strips[1]], inner0[leaf] + end0[leaf])
        part[leaf] = total + mul(inverse[leaf, :, strips[2]], across0[leaf] + end1[leaf])


def last_kernel(part, far_high, far_low, across1, end2, right, solved, small):
    for leaf in range(part.shape[0]):
        block = split(across1[leaf] + end2[leaf])
        total = part[leaf] + dot3((far_high[leaf], far_low[leaf]), block)
        solved[leaf] = total
        small[leaf] = mul(total, right[leaf], TN)


def spread_kernel(pieces, sent):
    for side in range(2):
        p = RUN * side
        total = pieces[p] + pieces[p + 1] + (pieces[p + 2] + pieces[p + 3])
        for q in range(RUN):
            sent[q, side] = total


def eliminate(matrix, joined):
    size = matrix.shape[0]
    row = lax.broadcasted_iota(jnp.int32, (size, size), 0)
    lane = lax.broadcasted_iota(jnp.int32, (size, size), 1)
    identity = (row == lane).astype(jnp.float32)
    joined[0] = matrix
    joined[1] = identity
    tall = lax.broadcasted_iota(jnp.int32, (size, 1), 0)

    def step(k, carry):
        used, picks = carry
        left = joined[0]
        column = jnp.sum(jnp.where(lane == k, left, 0.0), axis=1, keepdims=True)
        height = jnp.where(used > 0.0, -1.0, jnp.abs(column))
        best = jnp.max(height, axis=0, keepdims=True)
        pick = jnp.min(jnp.where(height == best, tall, size), axis=0, keepdims=True)
        chosen = tall == pick
        pivot = jnp.sum(jnp.where(chosen, column, 0.0), axis=0, keepdims=True)
        others = jnp.where(chosen, 0.0, column)
        for side in range(2):
            part = joined[side]
            pivot_row = jnp.sum(jnp.where(chosen, part, 0.0), axis=0, keepdims=True) / pivot
            joined[side] = jnp.where(chosen, pivot_row, part - others * pivot_row)
        picks = jnp.where(jnp.logical_and(chosen, lane == k), 1.0, picks)
        return jnp.where(chosen, 1.0, used), picks

    _, picks = lax.fori_loop(
        0, size, step, (jnp.zeros((size, 1), jnp.float32), jnp.zeros((size, size), jnp.float32))
    )
    return exact(picks, joined[1], TN)


def invert_kernel(gathered, inverse, power, joined):
    size = inverse.shape[0]
    first = gathered[:, 0].reshape(size, size)
    second = gathered[:, 1].reshape(size, size)
    row = lax.broadcasted_iota(jnp.int32, (size, size), 0)
    lane = lax.broadcasted_iota(jnp.int32, (size, size), 1)
    identity = (row == lane).astype(jnp.float32)
    start = exact(first, second)
    power[...] = start
    inverse[...] = identity + start

    def unsettled(state):
        count, norm = state
        going = jnp.logical_and(norm > SETTLED * SETTLED, norm < 1e12)
        return jnp.logical_and(count < DOUBLINGS, going)

    def double(state):
        count, _ = state
        current = split(power[...])
        square = dot3(current, current)
        power[...] = square
        held = inverse[...]
        inverse[...] = held + mul(held, square)
        return count + 1, jnp.sum(square * square)

    _, norm = lax.while_loop(unsettled, double, (jnp.int32(0), jnp.sum(start * start)))

    @pl.when(jnp.logical_not(norm <= SETTLED * SETTLED))
    def _():
        inverse[...] = eliminate(identity - exact(first, second), joined)


def coeffs_kernel(pieces, gathered, inverse, sent):
    size = inverse.shape[0]
    first = gathered[:, 0].reshape(size, size)
    second = gathered[:, 1].reshape(size, size)
    first_h = pieces[0] + pieces[1] + (pieces[2] + pieces[3])
    second_h = pieces[4] + pieces[5] + (pieces[6] + pieces[7])
    target = second_h - mul(first_h, second)
    first_c = mul(target, inverse[...])
    second_c = first_h - mul(first_c, first)
    for q in range(RUN):
        sent[q] = first_c
        sent[RUN + q] = second_c


def final_kernel(second, first, coeffs_t, out):
    for leaf in range(out.shape[0]):
        out[leaf] = second[leaf] - mul(first[leaf], coeffs_t[leaf], NT)


TO_INNER = [(0, 1), (RUN - 1, RUN - 2)]
TO_END = [(1, 0), (RUN - 2, RUN - 1)]
ACROSS = [(1, RUN - 2), (RUN - 2, 1)]


def move(shard, pairs):
    return lax.ppermute(shard, "col", pairs)


def body(leaf_inverse, left_gen, right_gen, parent_gen):
    leaves, rows, order_k = left_gen.shape
    quarter = order_k // RUN
    place = lax.axis_index("col").reshape(1).astype(jnp.int32)
    stride = 1 << LEVEL
    groups = [
        [side * RUN + q for side in (leaf, leaf ^ stride) for q in range(RUN)]
        for leaf in range(lax.axis_size("leaf"))
        if not leaf & stride
    ]
    f32, bf16 = jnp.float32, jnp.bfloat16
    both = ((leaves, rows, order_k), f32)
    small = ((leaves, order_k, order_k), f32)
    strips = ((leaves, rows, rows), bf16)
    square = ((order_k, order_k), f32)
    unit = 6 * rows * rows * order_k

    def exchange(value):
        return lax.all_to_all(value, ("leaf", "col"), 0, 0, axis_index_groups=groups, tiled=True)

    def near(weight, *gens):
        return call(
            near_kernel,
            "near",
            (both,),
            (place, leaf_inverse) + gens,
            weight * 6 * unit,
            scalars=1,
        )

    def last(weight, parts, *gens):
        return call(
            last_kernel, "last", (both, small), (*parts, *far, *gens, right_gen), weight * 4 * unit
        )

    far = call(
        fourth_kernel, "fourth", (strips, strips), (place, leaf_inverse), unit, scalars=1
    )
    inner0 = move(left_gen, TO_INNER)
    across0 = move(left_gen, ACROSS)
    end0 = move(left_gen, TO_END)
    across0, inner0, end0, parent = lax.optimization_barrier((across0, inner0, end0, parent_gen))
    across1 = move(inner0, ACROSS)
    end1 = move(across0, TO_END)
    inner0_p = move(parent, TO_INNER)
    across1, end1, parent = lax.optimization_barrier((across1, end1, parent))
    end2 = move(across1, TO_END)
    across0_p = move(parent, ACROSS)
    end0_p = move(parent, TO_END)
    near_g = near(1, left_gen, inner0, end0, across0, end1)
    first, small_g = last(1, near_g, across1, end2)

    across1_p = move(inner0_p, ACROSS)
    end1_p = move(across0_p, TO_END)
    end2_p = move(across1_p, TO_END)
    near_h = near(WEIGHT, parent_gen, inner0_p, end0_p, across0_p, end1_p)
    second, small_h = last(WEIGHT, near_h, across1_p, end2_p)

    pieces = exchange(small_g.reshape(2 * RUN, quarter, order_k))
    (spread,) = call(
        spread_kernel, "spread", (((RUN, 2, quarter, order_k), f32),), (pieces,), unit // 8
    )
    gathered = lax.all_to_all(spread, "col", 0, 0, tiled=True)
    (inverse,) = call(
        invert_kernel,
        "invert",
        (square,),
        (gathered,),
        10 * unit,
        scratch=(pltpu.VMEM(square[0], f32), pltpu.VMEM((2,) + square[0], f32)),
    )
    pieces_h = exchange(small_h.reshape(2 * RUN, quarter, order_k))
    (sent,) = call(
        coeffs_kernel, "coeffs", ((pieces_h.shape, f32),), (pieces_h, gathered, inverse), unit
    )
    coeffs_t = exchange(sent).reshape(leaves, order_k, order_k)
    (out,) = call(final_kernel, "final", (both,), (second, first, coeffs_t), 2 * unit)
    return out


def solution(mesh):
    return jax.shard_map(
        body,
        mesh=mesh,
        in_specs=(
            P("leaf", "col", None),
            P("leaf", "col", None),
            P("leaf", "col", None),
            P("leaf", "col", None),
        ),
        out_specs=P("leaf", "col", None),
        check_vma=False,
    )
```

```python
import functools

import jax
import jax.numpy as jnp
from jax import lax
from jax.experimental import pallas as pl
from jax.experimental.pallas import tpu as pltpu
from jax.sharding import PartitionSpec as P

LEVEL = 2
RUN = 4
NN = (((1,), (0,)), ((), ()))
NT = (((1,), (1,)), ((), ()))
TN = (((0,), (0,)), ((), ()))
PARAMS = pltpu.CompilerParams(vmem_limit_bytes=8 * 1024 * 1024)
SETTLED = 2.4e-4
DOUBLINGS = 9
WEIGHT = 40


def split(value):
    high = value.astype(jnp.bfloat16)
    low = (value - high.astype(jnp.float32)).astype(jnp.bfloat16)
    return high, low


def dot3(left, right, dims=NN):
    product = functools.partial(
        lax.dot_general, dimension_numbers=dims, preferred_element_type=jnp.float32
    )
    (lh, ll), (rh, rl) = left, right
    return product(lh, rh) + (product(lh, rl) + product(ll, rh))


def mul(left, right, dims=NN):
    return dot3(split(left), split(right), dims)


def exact(left, right, dims=NN):
    return lax.dot_general(
        left, right, dims, precision=lax.Precision.HIGHEST, preferred_element_type=jnp.float32
    )


def call(kernel, name, shapes, operands, flops, scalars=0, scratch=()):
    vmem = pl.BlockSpec(memory_space=pltpu.VMEM)
    smem = pl.BlockSpec(memory_space=pltpu.SMEM)
    return pl.pallas_call(
        kernel,
        out_shape=tuple(jax.ShapeDtypeStruct(shape, dtype) for shape, dtype in shapes),
        in_specs=[smem] * scalars + [vmem] * (len(operands) - scalars),
        out_specs=(vmem,) * len(shapes),
        scratch_shapes=list(scratch),
        compiler_params=PARAMS,
        cost_estimate=pl.CostEstimate(flops=flops, bytes_accessed=4 << 20, transcendentals=0),
        name=name,
    )(*operands)


def block_columns(c, rows):
    near_half = c < RUN // 2
    indices = (c, jnp.bitwise_xor(c, 1), jnp.where(near_half, 2, 1), jnp.where(near_half, 3, 0))
    return [pl.ds(pl.multiple_of(index * rows, rows), rows) for index in indices]


def near_kernel(place, inverse, own, inner0, end0, across0, end1, part, far_high, far_low):
    strips = block_columns(place[0], own.shape[1])
    for leaf in range(own.shape[0]):
        total = mul(inverse[leaf, :, strips[0]], own[leaf])
        total += mul(inverse[leaf, :, strips[1]], inner0[leaf] + end0[leaf])
        part[leaf] = total + mul(inverse[leaf, :, strips[2]], across0[leaf] + end1[leaf])
        far_high[leaf], far_low[leaf] = split(inverse[leaf, :, strips[3]])


def last_kernel(part, far_high, far_low, across1, end2, right, solved, small):
    for leaf in range(part.shape[0]):
        block = split(across1[leaf] + end2[leaf])
        total = part[leaf] + dot3((far_high[leaf], far_low[leaf]), block)
        solved[leaf] = total
        small[leaf] = mul(total, right[leaf], TN)


def spread_kernel(pieces, sent):
    for side in range(2):
        p = RUN * side
        total = pieces[p] + pieces[p + 1] + (pieces[p + 2] + pieces[p + 3])
        for q in range(RUN):
            sent[q, side] = total


def eliminate(matrix, joined):
    size = matrix.shape[0]
    row = lax.broadcasted_iota(jnp.int32, (size, size), 0)
    lane = lax.broadcasted_iota(jnp.int32, (size, size), 1)
    identity = (row == lane).astype(jnp.float32)
    joined[0] = matrix
    joined[1] = identity
    tall = lax.broadcasted_iota(jnp.int32, (size, 1), 0)

    def step(k, carry):
        used, picks = carry
        left = joined[0]
        column = jnp.sum(jnp.where(lane == k, left, 0.0), axis=1, keepdims=True)
        height = jnp.where(used > 0.0, -1.0, jnp.abs(column))
        best = jnp.max(height, axis=0, keepdims=True)
        pick = jnp.min(jnp.where(height == best, tall, size), axis=0, keepdims=True)
        chosen = tall == pick
        pivot = jnp.sum(jnp.where(chosen, column, 0.0), axis=0, keepdims=True)
        others = jnp.where(chosen, 0.0, column)
        for side in range(2):
            part = joined[side]
            pivot_row = jnp.sum(jnp.where(chosen, part, 0.0), axis=0, keepdims=True) / pivot
            joined[side] = jnp.where(chosen, pivot_row, part - others * pivot_row)
        picks = jnp.where(jnp.logical_and(chosen, lane == k), 1.0, picks)
        return jnp.where(chosen, 1.0, used), picks

    _, picks = lax.fori_loop(
        0, size, step, (jnp.zeros((size, 1), jnp.float32), jnp.zeros((size, size), jnp.float32))
    )
    return exact(picks, joined[1], TN)


def invert_kernel(gathered, inverse, power, joined):
    size = inverse.shape[0]
    first = gathered[:, 0].reshape(size, size)
    second = gathered[:, 1].reshape(size, size)
    row = lax.broadcasted_iota(jnp.int32, (size, size), 0)
    lane = lax.broadcasted_iota(jnp.int32, (size, size), 1)
    identity = (row == lane).astype(jnp.float32)
    start = exact(first, second)
    power[...] = start
    inverse[...] = identity + start

    def unsettled(state):
        count, norm = state
        going = jnp.logical_and(norm > SETTLED * SETTLED, norm < 1e12)
        return jnp.logical_and(count < DOUBLINGS, going)

    def double(state):
        count, _ = state
        current = split(power[...])
        square = dot3(current, current)
        power[...] = square
        held = inverse[...]
        inverse[...] = held + mul(held, square)
        return count + 1, jnp.sum(square * square)

    _, norm = lax.while_loop(unsettled, double, (jnp.int32(0), jnp.sum(start * start)))

    @pl.when(jnp.logical_not(norm <= SETTLED * SETTLED))
    def _():
        inverse[...] = eliminate(identity - exact(first, second), joined)


def coeffs_kernel(pieces, gathered, inverse, sent):
    size = inverse.shape[0]
    first = gathered[:, 0].reshape(size, size)
    second = gathered[:, 1].reshape(size, size)
    first_h = pieces[0] + pieces[1] + (pieces[2] + pieces[3])
    second_h = pieces[4] + pieces[5] + (pieces[6] + pieces[7])
    target = second_h - mul(first_h, second)
    first_c = mul(target, inverse[...])
    second_c = first_h - mul(first_c, first)
    for q in range(RUN):
        sent[q] = first_c
        sent[RUN + q] = second_c


def final_kernel(second, first, coeffs_t, out):
    for leaf in range(out.shape[0]):
        out[leaf] = second[leaf] - mul(first[leaf], coeffs_t[leaf], NT)


TO_INNER = [(0, 1), (RUN - 1, RUN - 2)]
TO_END = [(1, 0), (RUN - 2, RUN - 1)]
ACROSS = [(1, RUN - 2), (RUN - 2, 1)]


def move(shard, pairs):
    return lax.ppermute(shard, "col", pairs)


def body(leaf_inverse, left_gen, right_gen, parent_gen):
    leaves, rows, order_k = left_gen.shape
    quarter = order_k // RUN
    place = lax.axis_index("col").reshape(1).astype(jnp.int32)
    stride = 1 << LEVEL
    groups = [
        [side * RUN + q for side in (leaf, leaf ^ stride) for q in range(RUN)]
        for leaf in range(lax.axis_size("leaf"))
        if not leaf & stride
    ]
    f32, bf16 = jnp.float32, jnp.bfloat16
    both = ((leaves, rows, order_k), f32)
    small = ((leaves, order_k, order_k), f32)
    strips = ((leaves, rows, rows), bf16)
    square = ((order_k, order_k), f32)
    unit = 6 * rows * rows * order_k

    def exchange(value):
        return lax.all_to_all(value, ("leaf", "col"), 0, 0, axis_index_groups=groups, tiled=True)

    def near(weight, *gens):
        return call(
            near_kernel,
            "near",
            (both, strips, strips),
            (place, leaf_inverse) + gens,
            weight * 6 * unit,
            scalars=1,
        )

    def last(weight, parts, *gens):
        return call(
            last_kernel, "last", (both, small), (*parts, *gens, right_gen), weight * 4 * unit
        )

    inner0 = move(left_gen, TO_INNER)
    across0 = move(left_gen, ACROSS)
    end0 = move(left_gen, TO_END)
    inner0, across0, end0, parent = lax.optimization_barrier((inner0, across0, end0, parent_gen))
    across1 = move(inner0, ACROSS)
    end1 = move(across0, TO_END)
    inner0_p = move(parent, TO_INNER)
    across1, end1, parent = lax.optimization_barrier((across1, end1, parent))
    end2 = move(across1, TO_END)
    across0_p = move(parent, ACROSS)
    end0_p = move(parent, TO_END)
    near_g = near(1, left_gen, inner0, end0, across0, end1)
    first, small_g = last(1, near_g, across1, end2)

    across1_p = move(inner0_p, ACROSS)
    end1_p = move(across0_p, TO_END)
    end2_p = move(across1_p, TO_END)
    near_h = near(WEIGHT, parent_gen, inner0_p, end0_p, across0_p, end1_p)
    second, small_h = last(WEIGHT, near_h, across1_p, end2_p)

    pieces = exchange(small_g.reshape(2 * RUN, quarter, order_k))
    (spread,) = call(
        spread_kernel, "spread", (((RUN, 2, quarter, order_k), f32),), (pieces,), unit // 8
    )
    gathered = lax.all_to_all(spread, "col", 0, 0, tiled=True)
    (inverse,) = call(
        invert_kernel,
        "invert",
        (square,),
        (gathered,),
        10 * unit,
        scratch=(pltpu.VMEM(square[0], f32), pltpu.VMEM((2,) + square[0], f32)),
    )
    pieces_h = exchange(small_h.reshape(2 * RUN, quarter, order_k))
    (sent,) = call(
        coeffs_kernel, "coeffs", ((pieces_h.shape, f32),), (pieces_h, gathered, inverse), unit
    )
    coeffs_t = exchange(sent).reshape(leaves, order_k, order_k)
    (out,) = call(final_kernel, "final", (both,), (second, first, coeffs_t), 2 * unit)
    return out


def solution(mesh):
    return jax.shard_map(
        body,
        mesh=mesh,
        in_specs=(
            P("leaf", "col", None),
            P("leaf", "col", None),
            P("leaf", "col", None),
            P("leaf", "col", None),
        ),
        out_specs=P("leaf", "col", None),
        check_vma=False,
    )
```
